32 devices in a mesh: grp: 2 (over x), blk: 16 (over z, y, core).
Axes of the slice: x: 2, y: 2, z: 4, core: 2. Of those that a mesh axis runs over, the one named last changes fastest.
Arguments:
- tokens_act: bfloat16 [512, 8192], P(('grp', 'blk')), parts along dimension 0, may hold values from -6 to 6
- tokens_grad: bfloat16 [512, 28672], P(('grp', 'blk')), parts along dimension 0, may hold values from -6 to 6
- act_factors: bfloat16 [8192, 6144], P(None, ('grp', 'blk')), parts along dimension 1, may hold values from -0.0068359375 to 0.0068359375
- grad_factors: bfloat16 [28672, 6144], P(None, ('grp', 'blk')), parts along dimension 1, may hold values from -0.0034179688 to 0.0034179688
- act_eigen: float32 [8192], replicated, may hold values from 0.1 to 10
- grad_eigen: float32 [28672], replicated, may hold values from 0.1 to 10
- doc_lengths: int32 [32], P('grp'), parts along dimension 0, may hold values from 1 to 32, 256 in all
Outputs:
- scores: float32 [192, 16], P(('grp', 'blk')), parts along dimension 0
The draws below stay inside these ranges and needn't reach their ends.
There are 2 independent parts, one for each index of `grp`. The reference program is written for one: setup_inputs(seed, part) draws one part's arguments, and reference() takes and returns one part's arrays. A program takes and returns all parts, laid end to end along the dimension named above; an argument that names none is the same for every part. Nothing has to cross between parts.
Inputs may be any that keep to these rules, and one draw needn't show every extreme that they name: `doc_lengths`: the counts sum to 256.
All inputs are finite; a program needn't handle non-finite values.
Results may differ from the reference program's by a relative error of at most 0.0041.
Values may be sent and summed in bfloat16 or wider, within the bound.
A program may use at most 128 MiB of HBM per device.

```python
import math
import jax
import jax.numpy as jnp
import numpy as np
from jax import lax

DIN = 8192
DOUT = 28672
RANK = 32
DOCS = 16
QUERIES = 96
TOKENS = 256


def block_levels(rng, dims, split, smallest, largest):
    gain = 1.0
    for dim, blocks in split:
        draws = jax.random.uniform(jax.random.fold_in(jax.random.fold_in(rng, 6), dim), (blocks,), jnp.float32, smallest / len(split), largest / len(split))
        gain = gain * jnp.repeat(jnp.exp(draws), dims[dim] // blocks).reshape((-1,) + (1,) * (len(dims) - 1 - dim))
    return gain


def profile(amount, total, most, skew):
    loads = [(1 << 20) // math.isqrt(standing ** skew) + 1 for standing in range(2, amount + 1)]
    rest, holding = total - most - (amount - 1), [1] * (amount - 1)
    while rest > 0:
        free = [i for i in range(amount - 1) if holding[i] < most]
        mass, budget = sum([loads[i] for i in free]), rest
        for i in free:
            more = min(most - holding[i], max(1, budget * loads[i] // mass), rest)
            holding[i] = holding[i] + more
            rest = rest - more
    return np.array([most] + holding)


def ragged_sizes(key, count, total, limit, skew):
    if count == 2:
        one = jax.random.randint(key, (), max(1, total - limit), min(limit, total - 1) + 1)
        return jnp.stack([one, total - one])
    tallies = jnp.asarray(profile(count, total, limit, skew), jnp.int32)
    twos = (count - 1) // 2
    source_of, receiver = tallies[1:1 + 2 * twos:2], tallies[2:2 + 2 * twos:2]
    margin = jnp.minimum(source_of - 1, limit - receiver)
    shifted = jax.random.randint(jax.random.fold_in(key, 1), (twos,), 0, 1 << 20) % (margin + 1)
    tallies = tallies.at[1:1 + 2 * twos:2].set(source_of - shifted).at[2:2 + 2 * twos:2].set(receiver + shifted)
    return tallies[jax.random.permutation(jax.random.fold_in(key, 2), count)]


def bell_draw(rng, dims, scale, limit, cuts=(), held_as=jnp.bfloat16):
    factor_of = block_levels(rng, dims, cuts, -0.22, 0.18) if cuts else 1.0
    drawn = jax.random.normal(rng, dims, jnp.float32) * scale * factor_of
    return jnp.minimum(jnp.maximum(drawn, -limit), limit).astype(held_as)


def setup_inputs(seed: int = 0, part: int = 0) -> dict:
    splits = jax.random.split(jax.random.key(seed), 8)
    part_splits = jax.random.split(jax.random.fold_in(splits[7], part), 8)
    tokens_act = bell_draw(part_splits[0], (TOKENS, DIN), 1.0, 6.0, ((0, 16),))
    tokens_grad = bell_draw(part_splits[1], (TOKENS, DOUT), 1.0, 6.0, ((0, 16),))
    act_factors = bell_draw(part_splits[2], (DIN, QUERIES * RANK), (100 * DIN) ** -0.5, 0.0068359375, ((1, 16),))
    grad_factors = bell_draw(part_splits[3], (DOUT, QUERIES * RANK), (100 * DOUT) ** -0.5, 0.0034179688, ((1, 16),))
    act_eigen = jnp.clip(jnp.exp(jax.random.uniform(splits[4], (DIN,), jnp.float32, math.log(0.1), math.log(10.0))), 0.1, 10.0)
    grad_eigen = jnp.clip(jnp.exp(jax.random.uniform(splits[5], (DOUT,), jnp.float32, math.log(0.1), math.log(10.0))), 0.1, 10.0)
    doc_lengths = ragged_sizes(part_splits[6], DOCS, TOKENS, 2 * TOKENS // DOCS, 2).astype(jnp.int32)
    return dict(tokens_act=tokens_act, tokens_grad=tokens_grad, act_factors=act_factors, grad_factors=grad_factors, act_eigen=act_eigen, grad_eigen=grad_eigen, doc_lengths=doc_lengths)


def precondition(factors, eigen):
    damping = 0.1 * jnp.mean(eigen)
    return (factors.astype(jnp.float32) / (eigen + damping)[:, None]).astype(jnp.bfloat16)


def reference(tokens_act, tokens_grad, act_factors, grad_factors, act_eigen, grad_eigen, doc_lengths):
    act_pre = precondition(act_factors, act_eigen)
    grad_pre = precondition(grad_factors, grad_eigen)
    act_proj = jnp.dot(tokens_act, act_pre, preferred_element_type=jnp.float32)
    grad_proj = jnp.dot(tokens_grad, grad_pre, preferred_element_type=jnp.float32)
    per_token = (act_proj * grad_proj).reshape(TOKENS, QUERIES, RANK).sum(axis=2)
    doc_ends = jnp.cumsum(doc_lengths).astype(jnp.int32)
    doc_starts = doc_ends - doc_lengths.astype(jnp.int32)
    token_index = jnp.arange(TOKENS, dtype=jnp.int32)
    member = ((token_index[None, :] >= doc_starts[:, None]) & (token_index[None, :] < doc_ends[:, None])).astype(jnp.float32)
    totals = jnp.dot(member, per_token, precision=lax.Precision.HIGHEST, preferred_element_type=jnp.float32)
    return totals.T
```

```python
import functools

import jax
import jax.numpy as jnp
from jax import lax
from jax.experimental import pallas as pl
from jax.experimental.pallas import tpu as pltpu
from jax.sharding import PartitionSpec as P

RANK = 32
CHUNK = 2048
LAG = 1
SWAP_FIRST = (6, 3)
RAW = 3
MESH = pl.DeviceIdType.MESH


def kernel(
    lines, tok_act, tok_grad, fac_act, fac_grad, eig_act, eig_grad, lengths, out,
    gat, raw, pre, recip, acc, load_sem, raw_sem, recv_sem, send_sem,
):
    chunks, tokens, width = gat.shape
    rows = tok_act.shape[0]
    count = tokens // rows
    depth = count // (2 * lines)
    act_chunks = tok_act.shape[1] // width
    me = lax.axis_index("blk")
    core = me % 2
    line = (me // 2) % lines
    place = me // (2 * lines)

    def block(at, ln, co):
        return (at * lines + ln) * 2 + co

    ahead, behind = block(place + 1, line, core), block(place - 1, line, core)
    across, sibling = block(place, lines - 1 - line, core), block(place, line, 1 - core)
    has_ahead, has_behind = place < depth - 1, place > 0

    def piece(c, owner):
        return gat.at[c, pl.ds(pl.multiple_of(owner * rows, rows), rows), :]

    def copy(link, c, owner, target):
        ref = piece(c, owner)
        return pltpu.make_async_remote_copy(
            src_ref=ref, dst_ref=ref,
            send_sem=send_sem.at[link, c, owner // 2], recv_sem=recv_sem.at[c, owner],
            device_id={"blk": target}, device_id_type=MESH,
        )

    def arrived(c, owner):
        copy(0, c, owner, sibling).wait_recv()

    for c in range(chunks):
        if c < act_chunks:
            source = tok_act.at[:, pl.ds(c * width, width)]
        else:
            source = tok_grad.at[:, pl.ds((c - act_chunks) * width, width)]
        pltpu.make_async_copy(source, piece(c, me), load_sem.at[c]).start()

    def fetch(p):
        slot = raw.at[lax.rem(p, RAW)]
        sem = raw_sem.at[lax.rem(p, RAW)]

        @pl.when(p < act_chunks)
        def _():
            at = pl.multiple_of(p * width, width)
            pltpu.make_async_copy(fac_act.at[pl.ds(at, width), :], slot, sem).start()

        @pl.when((p >= act_chunks) & (p < chunks))
        def _():
            at = pl.multiple_of((p - act_chunks) * width, width)
            pltpu.make_async_copy(fac_grad.at[pl.ds(at, width), :], slot, sem).start()

    for p in range(RAW):
        fetch(jnp.int32(p))

    barrier = pltpu.get_barrier_semaphore()
    friends = [(sibling, True), (ahead, has_ahead), (behind, has_behind)]
    if lines > 1:
        friends.append((across, True))
    for friend, there in friends:
        @pl.when(there)
        def _(friend=friend):
            pl.semaphore_signal(barrier, inc=1, device_id={"blk": friend}, device_id_type=MESH)
    ends_of_line = (place == 0).astype(jnp.int32) + (place == depth - 1).astype(jnp.int32)
    pl.semaphore_wait(barrier, len(friends) - ends_of_line)

    def swaps_first(c):
        return lax.rem(c, SWAP_FIRST[0]) == SWAP_FIRST[1]

    def sends(c, apart, side, same, act):
        at = place + side * apart
        ln = line if same else lines - 1 - line
        owner = block(at, ln, core)
        act(3, sibling, True, owner)
        along = True if same else swaps_first(c)
        if side <= 0:
            act(0, ahead, has_ahead & along, owner)
        if side >= 0:
            act(1, behind, has_behind & along, owner)
        if same and lines > 1:
            act(2, across, True if apart == 0 else jnp.logical_not(swaps_first(c)), owner)

    hops = []
    for same in ((True, False) if lines > 1 else (True,)):
        for apart in range(depth):
            for side in ((0,) if apart == 0 else (-1, 1)):
                hops.append((apart + (0 if same else 1), apart, side, same))
    hops.sort(key=lambda hop: hop[0])
    last_hop = depth - 1 + (1 if lines > 1 else 0) + 1

    def in_reach(apart, side):
        if side == 0:
            return True
        return (place >= apart) if side < 0 else (place + apart < depth)

    def forward(s):
        for hop, apart, side, same in hops:
            c = s - LAG * hop

            @pl.when((c >= 0) & (c < chunks) & in_reach(apart, side))
            def _(hop=hop, apart=apart, side=side, same=same, c=c):
                owner = block(place + side * apart, line if same else lines - 1 - line, core)
                if hop == 0:
                    pltpu.make_async_copy(
                        tok_act.at[:, pl.ds(0, width)], piece(c, me), load_sem.at[c]
                    ).wait()
                else:
                    arrived(c, owner)

                def act(link, target, when, owner):
                    @pl.when(when)
                    def _():
                        copy(link, c, owner, target).start()

                sends(c, apart, side, same, act)

    def drain(c):
        for hop, apart, side, same in hops:
            @pl.when(in_reach(apart, side))
            def _(apart=apart, side=side, same=same):
                def act(link, target, when, owner):
                    @pl.when(when)
                    def _():
                        copy(link, c, owner, target).wait_send()

                sends(c, apart, side, same, act)

    parts = eig_act.shape[0]
    for ref, first, n in ((eig_act, 0, parts), (eig_grad, parts, eig_grad.shape[0])):
        eigen = ref[...]
        damping = 0.1 * (jnp.sum(eigen, keepdims=True) / (n * 128))
        recip[pl.ds(first, n), :] = 1.0 / (eigen + damping)
    acc[...] = jnp.zeros_like(acc)
    columns = raw.shape[2]
    per_chunk = width // 128

    def precondition(p):
        slot = lax.rem(p, RAW)
        pltpu.make_async_copy(
            fac_act.at[pl.ds(0, width), :], raw.at[slot], raw_sem.at[slot]
        ).wait()

        def body(i, _):
            at = pl.multiple_of(i * 128, 128)
            row = recip[pl.ds(p * per_chunk + i, 1), :]
            scale = jnp.broadcast_to(row, (128, 128)).T
            for left in range(0, columns, 128):
                n = min(128, columns - left)
                part = raw[slot, pl.ds(at, 128), pl.ds(left, n)].astype(jnp.float32)
                pre[p % 2, pl.ds(at, 128), pl.ds(left, n)] = (part * scale[:, :n]).astype(jnp.bfloat16)
            return 0

        lax.fori_loop(0, per_chunk, body, 0)
        fetch(p + RAW)

    def multiply(c):
        for at in range(depth):
            for ln in range(lines):
                arrived(c, block(at, ln, 1 - core))
        which = (c >= act_chunks).astype(jnp.int32)
        acc[which] += jnp.dot(gat[c], pre[c % 2], preferred_element_type=jnp.float32)

    def step(s, _):
        forward(s)
        p = s - LAG * last_hop + 1

        @pl.when((p >= 0) & (p < chunks))
        def _():
            precondition(p)

        c = s - LAG * last_hop

        @pl.when(c >= 0)
        def _():
            multiply(c)

        return 0

    lax.fori_loop(0, chunks + LAG * last_hop, step, 0)

    docs = lengths.shape[1]
    queries = columns // RANK
    lens = jnp.broadcast_to(lengths[...].astype(jnp.float32), (docs, docs))
    down = lax.broadcasted_iota(jnp.int32, (docs, docs), 0)
    over = lax.broadcasted_iota(jnp.int32, (docs, docs), 1)
    ends = jnp.sum(jnp.where(over <= down, lens, 0.0), axis=1, keepdims=True)
    starts = jnp.sum(jnp.where(over < down, lens, 0.0), axis=1, keepdims=True)
    index = lax.broadcasted_iota(jnp.int32, (docs, tokens), 1).astype(jnp.float32)
    member = jnp.where((index >= starts) & (index < ends), 1.0, 0.0)
    product = acc[0] * acc[1]
    by_doc = jnp.dot(
        member, product, precision=lax.Precision.HIGHEST, preferred_element_type=jnp.float32
    )
    query = lax.broadcasted_iota(jnp.int32, (queries, columns), 0)
    column = lax.broadcasted_iota(jnp.int32, (queries, columns), 1)
    chosen = jnp.where((column >= query * RANK) & (column < query * RANK + RANK), 1.0, 0.0)
    out[...] = lax.dot_general(
        chosen, by_doc, (((1,), (1,)), ((), ())),
        precision=lax.Precision.HIGHEST, preferred_element_type=jnp.float32,
    )

    def drain_step(c, _):
        drain(c)
        return 0

    lax.fori_loop(0, chunks, drain_step, 0)


def local(lines, count, tok_act, tok_grad, fac_act, fac_grad, eig_act, eig_grad, lengths):
    rows, din = tok_act.shape
    dout = tok_grad.shape[1]
    columns = fac_act.shape[1]
    docs = lengths.shape[0]
    chunks = (din + dout) // CHUNK
    tokens = rows * count
    anywhere = pl.BlockSpec(memory_space=pl.ANY)
    vmem = pl.BlockSpec(memory_space=pltpu.VMEM)
    return pl.pallas_call(
        functools.partial(kernel, lines),
        out_shape=jax.ShapeDtypeStruct((columns // RANK, docs), jnp.float32),
        in_specs=[anywhere] * 4 + [vmem] * 3,
        out_specs=vmem,
        scratch_shapes=[
            pltpu.VMEM((chunks, tokens, CHUNK), jnp.bfloat16),
            pltpu.VMEM((RAW, CHUNK, columns), jnp.bfloat16),
            pltpu.VMEM((2, CHUNK, columns), jnp.bfloat16),
            pltpu.VMEM(((din + dout) // 128, 128), jnp.float32),
            pltpu.VMEM((2, tokens, columns), jnp.float32),
            pltpu.SemaphoreType.DMA((chunks,)),
            pltpu.SemaphoreType.DMA((RAW,)),
            pltpu.SemaphoreType.DMA((chunks, count)),
            pltpu.SemaphoreType.DMA((4, chunks, count // 2)),
        ],
        compiler_params=pltpu.CompilerParams(
            collective_id=0, has_side_effects=True, vmem_limit_bytes=60 * 2**20
        ),
    )(
        tok_act, tok_grad, fac_act, fac_grad,
        eig_act.reshape(-1, 128), eig_grad.reshape(-1, 128), lengths.reshape(1, docs),
    )


def solution(mesh):
    placed = (
        P(("grp", "blk"), None),
        P(("grp", "blk"), None),
        P(None, ("grp", "blk")),
        P(None, ("grp", "blk")),
        P(),
        P(),
        P("grp"),
    )
    count = mesh.shape["blk"]
    lines = 2 if count == 16 else 1
    return jax.shard_map(
        functools.partial(local, lines, count),
        mesh=mesh, in_specs=placed, out_specs=P(("grp", "blk"), None), check_vma=False,
    )
```

```python
import functools

import jax
import jax.numpy as jnp
from jax import lax
from jax.experimental import pallas as pl
from jax.experimental.pallas import tpu as pltpu
from jax.sharding import PartitionSpec as P

RANK = 32
CHUNK = 4096
LAG = 1
SWAP_FIRST = (5, 2)
RAW = 3
MESH = pl.DeviceIdType.MESH


def kernel(
    lines, tok_act, tok_grad, fac_act, fac_grad, eig_act, eig_grad, lengths, out,
    gat, raw, pre, recip, acc, load_sem, raw_sem, recv_sem, send_sem,
):
    chunks, tokens, width = gat.shape
    rows = tok_act.shape[0]
    count = tokens // rows
    depth = count // (2 * lines)
    act_chunks = tok_act.shape[1] // width
    me = lax.axis_index("blk")
    core = me % 2
    line = (me // 2) % lines
    place = me // (2 * lines)

    def block(at, ln, co):
        return (at * lines + ln) * 2 + co

    ahead, behind = block(place + 1, line, core), block(place - 1, line, core)
    across, sibling = block(place, lines - 1 - line, core), block(place, line, 1 - core)
    has_ahead, has_behind = place < depth - 1, place > 0

    def piece(c, owner):
        return gat.at[c, pl.ds(pl.multiple_of(owner * rows, rows), rows), :]

    def copy(link, c, owner, target):
        ref = piece(c, owner)
        return pltpu.make_async_remote_copy(
            src_ref=ref, dst_ref=ref,
            send_sem=send_sem.at[link, c, owner // 2], recv_sem=recv_sem.at[c, owner],
            device_id={"blk": target}, device_id_type=MESH,
        )

    def arrived(c, owner):
        copy(0, c, owner, sibling).wait_recv()

    for c in range(chunks):
        if c < act_chunks:
            source = tok_act.at[:, pl.ds(c * width, width)]
        else:
            source = tok_grad.at[:, pl.ds((c - act_chunks) * width, width)]
        pltpu.make_async_copy(source, piece(c, me), load_sem.at[c]).start()

    def fetch(p):
        slot = raw.at[lax.rem(p, RAW)]
        sem = raw_sem.at[lax.rem(p, RAW)]

        @pl.when(p < act_chunks)
        def _():
            at = pl.multiple_of(p * width, width)
            pltpu.make_async_copy(fac_act.at[:, pl.ds(at, width)], slot, sem).start()

        @pl.when((p >= act_chunks) & (p < chunks))
        def _():
            at = pl.multiple_of((p - act_chunks) * width, width)
            pltpu.make_async_copy(fac_grad.at[:, pl.ds(at, width)], slot, sem).start()

    for p in range(RAW):
        fetch(jnp.int32(p))

    barrier = pltpu.get_barrier_semaphore()
    friends = [(sibling, True), (ahead, has_ahead), (behind, has_behind)]
    if lines > 1:
        friends.append((across, True))
    for friend, there in friends:
        @pl.when(there)
        def _(friend=friend):
            pl.semaphore_signal(barrier, inc=1, device_id={"blk": friend}, device_id_type=MESH)
    ends_of_line = (place == 0).astype(jnp.int32) + (place == depth - 1).astype(jnp.int32)
    pl.semaphore_wait(barrier, len(friends) - ends_of_line)

    def swaps_first(c):
        return lax.rem(c, SWAP_FIRST[0]) == SWAP_FIRST[1]

    def sends(c, apart, side, same, act):
        at = place + side * apart
        ln = line if same else lines - 1 - line
        owner = block(at, ln, core)
        act(3, sibling, True, owner)
        along = True if same else swaps_first(c)
        if side <= 0:
            act(0, ahead, has_ahead & along, owner)
        if side >= 0:
            act(1, behind, has_behind & along, owner)
        if same and lines > 1:
            act(2, across, True if apart == 0 else jnp.logical_not(swaps_first(c)), owner)

    hops = []
    for same in ((True, False) if lines > 1 else (True,)):
        for apart in range(depth):
            for side in ((0,) if apart == 0 else (-1, 1)):
                hops.append((apart + (0 if same else 1), apart, side, same))
    hops.sort(key=lambda hop: hop[0])
    last_hop = depth - 1 + (1 if lines > 1 else 0) + 1

    def in_reach(apart, side):
        if side == 0:
            return True
        return (place >= apart) if side < 0 else (place + apart < depth)

    def forward(s):
        for hop, apart, side, same in hops:
            c = s - LAG * hop

            @pl.when((c >= 0) & (c < chunks) & in_reach(apart, side))
            def _(hop=hop, apart=apart, side=side, same=same, c=c):
                owner = block(place + side * apart, line if same else lines - 1 - line, core)
                if hop == 0:
                    pltpu.make_async_copy(
                        tok_act.at[:, pl.ds(0, width)], piece(c, me), load_sem.at[c]
                    ).wait()
                else:
                    arrived(c, owner)

                def act(link, target, when, owner):
                    @pl.when(when)
                    def _():
                        copy(link, c, owner, target).start()

                sends(c, apart, side, same, act)

    def drain(c):
        for hop, apart, side, same in hops:
            @pl.when(in_reach(apart, side))
            def _(apart=apart, side=side, same=same):
                def act(link, target, when, owner):
                    @pl.when(when)
                    def _():
                        copy(link, c, owner, target).wait_send()

                sends(c, apart, side, same, act)

    parts = eig_act.shape[0]
    for ref, first, n in ((eig_act, 0, parts), (eig_grad, parts, eig_grad.shape[0])):
        eigen = ref[...]
        damping = 0.1 * (jnp.sum(eigen, keepdims=True) / (n * 128))
        recip[pl.ds(first, n), :] = 1.0 / (eigen + damping)
    acc[...] = jnp.zeros_like(acc)
    columns = raw.shape[1]
    per_chunk = width // 128

    def precondition(p):
        slot = lax.rem(p, RAW)
        pltpu.make_async_copy(
            fac_act.at[:, pl.ds(0, width)], raw.at[slot], raw_sem.at[slot]
        ).wait()

        def body(i, _):
            at = pl.multiple_of(i * 128, 128)
            row = recip[pl.ds(p * per_chunk + i, 1), :]
            part = raw[slot, :, pl.ds(at, 128)].astype(jnp.float32)
            pre[p % 2, :, pl.ds(at, 128)] = (part * row).astype(jnp.bfloat16)
            return 0

        lax.fori_loop(0, per_chunk, body, 0)
        fetch(p + RAW)

    def multiply(c):
        for at in range(depth):
            for ln in range(lines):
                arrived(c, block(at, ln, 1 - core))
        which = (c >= act_chunks).astype(jnp.int32)
        acc[which] += lax.dot_general(
            gat[c], pre[c % 2], (((1,), (1,)), ((), ())), preferred_element_type=jnp.float32
        )

    def step(s, _):
        forward(s)
        p = s - LAG * last_hop + 1

        @pl.when((p >= 0) & (p < chunks))
        def _():
            precondition(p)

        c = s - LAG * last_hop

        @pl.when(c >= 0)
        def _():
            multiply(c)

        return 0

    lax.fori_loop(0, chunks + LAG * last_hop, step, 0)

    docs = lengths.shape[1]
    queries = columns // RANK
    lens = jnp.broadcast_to(lengths[...].astype(jnp.float32), (docs, docs))
    down = lax.broadcasted_iota(jnp.int32, (docs, docs), 0)
    over = lax.broadcasted_iota(jnp.int32, (docs, docs), 1)
    ends = jnp.sum(jnp.where(over <= down, lens, 0.0), axis=1, keepdims=True)
    starts = jnp.sum(jnp.where(over < down, lens, 0.0), axis=1, keepdims=True)
    index = lax.broadcasted_iota(jnp.int32, (docs, tokens), 1).astype(jnp.float32)
    member = jnp.where((index >= starts) & (index < ends), 1.0, 0.0)
    product = acc[0] * acc[1]
    by_doc = jnp.dot(
        member, product, precision=lax.Precision.HIGHEST, preferred_element_type=jnp.float32
    )
    query = lax.broadcasted_iota(jnp.int32, (queries, columns), 0)
    column = lax.broadcasted_iota(jnp.int32, (queries, columns), 1)
    chosen = jnp.where((column >= query * RANK) & (column < query * RANK + RANK), 1.0, 0.0)
    out[...] = lax.dot_general(
        chosen, by_doc, (((1,), (1,)), ((), ())),
        precision=lax.Precision.HIGHEST, preferred_element_type=jnp.float32,
    )

    def drain_step(c, _):
        drain(c)
        return 0

    lax.fori_loop(0, chunks, drain_step, 0)


def local(lines, count, tok_act, tok_grad, fac_act, fac_grad, eig_act, eig_grad, lengths):
    fac_act, fac_grad = fac_act.T, fac_grad.T
    rows, din = tok_act.shape
    dout = tok_grad.shape[1]
    columns = fac_act.shape[0]
    docs = lengths.shape[0]
    chunks = (din + dout) // CHUNK
    tokens = rows * count
    anywhere = pl.BlockSpec(memory_space=pl.ANY)
    vmem = pl.BlockSpec(memory_space=pltpu.VMEM)
    return pl.pallas_call(
        functools.partial(kernel, lines),
        out_shape=jax.ShapeDtypeStruct((columns // RANK, docs), jnp.float32),
        in_specs=[anywhere] * 4 + [vmem] * 3,
        out_specs=vmem,
        scratch_shapes=[
            pltpu.VMEM((chunks, tokens, CHUNK), jnp.bfloat16),
            pltpu.VMEM((RAW, columns, CHUNK), jnp.bfloat16),
            pltpu.VMEM((2, columns, CHUNK), jnp.bfloat16),
            pltpu.VMEM(((din + dout) // 128, 128), jnp.float32),
            pltpu.VMEM((2, tokens, columns), jnp.float32),
            pltpu.SemaphoreType.DMA((chunks,)),
            pltpu.SemaphoreType.DMA((RAW,)),
            pltpu.SemaphoreType.DMA((chunks, count)),
            pltpu.SemaphoreType.DMA((4, chunks, count // 2)),
        ],
        compiler_params=pltpu.CompilerParams(
            collective_id=0, has_side_effects=True, vmem_limit_bytes=60 * 2**20
        ),
    )(
        tok_act, tok_grad, fac_act, fac_grad,
        eig_act.reshape(-1, 128), eig_grad.reshape(-1, 128), lengths.reshape(1, docs),
    )


def solution(mesh):
    placed = (
        P(("grp", "blk"), None),
        P(("grp", "blk"), None),
        P(None, ("grp", "blk")),
        P(None, ("grp", "blk")),
        P(),
        P(),
        P("grp"),
    )
    count = mesh.shape["blk"]
    lines = 2 if count == 16 else 1
    return jax.shard_map(
        functools.partial(local, lines, count),
        mesh=mesh, in_specs=placed, out_specs=P(("grp", "blk"), None), check_vma=False,
    )
```

```python
import functools

import jax
import jax.numpy as jnp
from jax import lax
from jax.experimental import pallas as pl
from jax.experimental.pallas import tpu as pltpu
from jax.sharding import PartitionSpec as P

RANK = 32
CHUNK = 4096
LAG = 1
SWAP_FIRST = (6, 1, 0)
RAW = 3
MESH = pl.DeviceIdType.MESH


def kernel(
    lines, tok_act, tok_grad, fac_act, fac_grad, eig_act, eig_grad, lengths, out,
    gat, raw, pre, recip, acc, load_sem, raw_sem, recv_sem, send_sem,
):
    chunks, tokens, width = gat.shape
    rows = tok_act.shape[0]
    count = tokens // rows
    depth = count // (2 * lines)
    act_chunks = tok_act.shape[1] // width
    me = lax.axis_index("blk")
    core = me % 2
    line = (me // 2) % lines
    place = me // (2 * lines)

    def block(at, ln, co):
        return (at * lines + ln) * 2 + co

    ahead, behind = block(place + 1, line, core), block(place - 1, line, core)
    across, sibling = block(place, lines - 1 - line, core), block(place, line, 1 - core)
    has_ahead, has_behind = place < depth - 1, place > 0

    def piece(c, owner):
        return gat.at[c, pl.ds(pl.multiple_of(owner * rows, rows), rows), :]

    def copy(link, c, owner, target):
        ref = piece(c, owner)
        return pltpu.make_async_remote_copy(
            src_ref=ref, dst_ref=ref,
            send_sem=send_sem.at[link, c, owner // 2], recv_sem=recv_sem.at[c, owner],
            device_id={"blk": target}, device_id_type=MESH,
        )

    def arrived(c, owner):
        copy(0, c, owner, sibling).wait_recv()

    for c in range(chunks):
        if c < act_chunks:
            source = tok_act.at[:, pl.ds(c * width, width)]
        else:
            source = tok_grad.at[:, pl.ds((c - act_chunks) * width, width)]
        pltpu.make_async_copy(source, piece(c, me), load_sem.at[c]).start()

    def fetch(p):
        slot = raw.at[lax.rem(p, RAW)]
        sem = raw_sem.at[lax.rem(p, RAW)]

        @pl.when(p < act_chunks)
        def _():
            at = pl.multiple_of(p * width, width)
            pltpu.make_async_copy(fac_act.at[:, pl.ds(at, width)], slot, sem).start()

        @pl.when((p >= act_chunks) & (p < chunks))
        def _():
            at = pl.multiple_of((p - act_chunks) * width, width)
            pltpu.make_async_copy(fac_grad.at[:, pl.ds(at, width)], slot, sem).start()

    for p in range(RAW):
        fetch(jnp.int32(p))

    barrier = pltpu.get_barrier_semaphore()
    friends = [(sibling, True), (ahead, has_ahead), (behind, has_behind)]
    if lines > 1:
        friends.append((across, True))
    for friend, there in friends:
        @pl.when(there)
        def _(friend=friend):
            pl.semaphore_signal(barrier, inc=1, device_id={"blk": friend}, device_id_type=MESH)
    ends_of_line = (place == 0).astype(jnp.int32) + (place == depth - 1).astype(jnp.int32)
    pl.semaphore_wait(barrier, len(friends) - ends_of_line)

    def swaps_first(c, at):
        return lax.rem(c + SWAP_FIRST[1] * (at + depth * core), SWAP_FIRST[0]) == SWAP_FIRST[2]

    def sends(c, apart, side, same, act):
        at = place + side * apart
        ln = line if same else lines - 1 - line
        owner = block(at, ln, core)
        along = True if same else swaps_first(c, at)
        if side <= 0:
            act(0, ahead, has_ahead & along, owner)
        if side >= 0:
            act(1, behind, has_behind & along, owner)
        if same and lines > 1:
            act(2, across, True if apart == 0 else jnp.logical_not(swaps_first(c, at)), owner)
        act(3, sibling, True, owner)

    hops = []
    for same in ((True, False) if lines > 1 else (True,)):
        for apart in range(depth):
            for side in ((0,) if apart == 0 else (-1, 1)):
                hops.append((apart + (0 if same else 1), apart, side, same))
    hops.sort(key=lambda hop: hop[0])
    last_hop = depth - 1 + (1 if lines > 1 else 0) + 1

    def in_reach(apart, side):
        if side == 0:
            return True
        return (place >= apart) if side < 0 else (place + apart < depth)

    def forward(s):
        for hop, apart, side, same in hops:
            c = s - LAG * hop

            @pl.when((c >= 0) & (c < chunks) & in_reach(apart, side))
            def _(hop=hop, apart=apart, side=side, same=same, c=c):
                owner = block(place + side * apart, line if same else lines - 1 - line, core)
                if hop == 0:
                    pltpu.make_async_copy(
                        tok_act.at[:, pl.ds(0, width)], piece(c, me), load_sem.at[c]
                    ).wait()
                else:
                    arrived(c, owner)

                def act(link, target, when, owner):
                    @pl.when(when)
                    def _():
                        copy(link, c, owner, target).start()

                sends(c, apart, side, same, act)

    def drain(c):
        for hop, apart, side, same in hops:
            @pl.when(in_reach(apart, side))
            def _(apart=apart, side=side, same=same):
                def act(link, target, when, owner):
                    @pl.when(when)
                    def _():
                        copy(link, c, owner, target).wait_send()

                sends(c, apart, side, same, act)

    parts = eig_act.shape[0]
    for ref, first, n in ((eig_act, 0, parts), (eig_grad, parts, eig_grad.shape[0])):
        eigen = ref[...]
        damping = 0.1 * (jnp.sum(eigen, keepdims=True) / (n * 128))
        recip[pl.ds(first, n), :] = 1.0 / (eigen + damping)
    acc[...] = jnp.zeros_like(acc)
    columns = raw.shape[1]
    per_chunk = width // 128

    def precondition(p):
        slot = lax.rem(p, RAW)
        pltpu.make_async_copy(
            fac_act.at[:, pl.ds(0, width)], raw.at[slot], raw_sem.at[slot]
        ).wait()

        def body(i, _):
            at = pl.multiple_of(i * 128, 128)
            row = recip[pl.ds(p * per_chunk + i, 1), :]
            part = raw[slot, :, pl.ds(at, 128)].astype(jnp.float32)
            pre[p % 2, :, pl.ds(at, 128)] = (part * row).astype(jnp.bfloat16)
            return 0

        lax.fori_loop(0, per_chunk, body, 0)
        fetch(p + RAW)

    def multiply(c):
        for at in range(depth):
            for ln in range(lines):
                arrived(c, block(at, ln, 1 - core))
        which = (c >= act_chunks).astype(jnp.int32)
        acc[which] += lax.dot_general(
            gat[c], pre[c % 2], (((1,), (1,)), ((), ())), preferred_element_type=jnp.float32
        )

    def step(s, _):
        forward(s)
        p = s - LAG * last_hop + 1

        @pl.when((p >= 0) & (p < chunks))
        def _():
            precondition(p)

        c = s - LAG * last_hop

        @pl.when(c >= 0)
        def _():
            multiply(c)

        return 0

    lax.fori_loop(0, chunks + LAG * last_hop, step, 0)

    docs = lengths.shape[1]
    queries = columns // RANK
    lens = jnp.broadcast_to(lengths[...].astype(jnp.float32), (docs, docs))
    down = lax.broadcasted_iota(jnp.int32, (docs, docs), 0)
    over = lax.broadcasted_iota(jnp.int32, (docs, docs), 1)
    ends = jnp.sum(jnp.where(over <= down, lens, 0.0), axis=1, keepdims=True)
    starts = jnp.sum(jnp.where(over < down, lens, 0.0), axis=1, keepdims=True)
    index = lax.broadcasted_iota(jnp.int32, (docs, tokens), 1).astype(jnp.float32)
    member = jnp.where((index >= starts) & (index < ends), 1.0, 0.0)
    product = acc[0] * acc[1]
    by_doc = jnp.dot(
        member, product, precision=lax.Precision.HIGHEST, preferred_element_type=jnp.float32
    )
    query = lax.broadcasted_iota(jnp.int32, (queries, columns), 0)
    column = lax.broadcasted_iota(jnp.int32, (queries, columns), 1)
    chosen = jnp.where((column >= query * RANK) & (column < query * RANK + RANK), 1.0, 0.0)
    out[...] = lax.dot_general(
        chosen, by_doc, (((1,), (1,)), ((), ())),
        precision=lax.Precision.HIGHEST, preferred_element_type=jnp.float32,
    )

    def drain_step(c, _):
        drain(c)
        return 0

    lax.fori_loop(0, chunks, drain_step, 0)


def local(lines, count, tok_act, tok_grad, fac_act, fac_grad, eig_act, eig_grad, lengths):
    fac_act, fac_grad = fac_act.T, fac_grad.T
    rows, din = tok_act.shape
    dout = tok_grad.shape[1]
    columns = fac_act.shape[0]
    docs = lengths.shape[0]
    chunks = (din + dout) // CHUNK
    tokens = rows * count
    anywhere = pl.BlockSpec(memory_space=pl.ANY)
    vmem = pl.BlockSpec(memory_space=pltpu.VMEM)
    return pl.pallas_call(
        functools.partial(kernel, lines),
        out_shape=jax.ShapeDtypeStruct((columns // RANK, docs), jnp.float32),
        in_specs=[anywhere] * 4 + [vmem] * 3,
        out_specs=vmem,
        scratch_shapes=[
            pltpu.VMEM((chunks, tokens, CHUNK), jnp.bfloat16),
            pltpu.VMEM((RAW, columns, CHUNK), jnp.bfloat16),
            pltpu.VMEM((2, columns, CHUNK), jnp.bfloat16),
            pltpu.VMEM(((din + dout) // 128, 128), jnp.float32),
            pltpu.VMEM((2, tokens, columns), jnp.float32),
            pltpu.SemaphoreType.DMA((chunks,)),
            pltpu.SemaphoreType.DMA((RAW,)),
            pltpu.SemaphoreType.DMA((chunks, count)),
            pltpu.SemaphoreType.DMA((4, chunks, count // 2)),
        ],
        compiler_params=pltpu.CompilerParams(
            collective_id=0, has_side_effects=True, vmem_limit_bytes=60 * 2**20
        ),
    )(
        tok_act, tok_grad, fac_act, fac_grad,
        eig_act.reshape(-1, 128), eig_grad.reshape(-1, 128), lengths.reshape(1, docs),
    )


def solution(mesh):
    placed = (
        P(("grp", "blk"), None),
        P(("grp", "blk"), None),
        P(None, ("grp", "blk")),
        P(None, ("grp", "blk")),
        P(),
        P(),
        P("grp"),
    )
    count = mesh.shape["blk"]
    lines = 2 if count == 16 else 1
    return jax.shard_map(
        functools.partial(local, lines, count),
        mesh=mesh, in_specs=placed, out_specs=P(("grp", "blk"), None), check_vma=False,
    )
```
